128 devices in a mesh: slab: 32 (over x, z, core), gy: 4 (over y).
Axes of the slice: x: 4, y: 4, z: 4, core: 2. Of those that a mesh axis runs over, the one named last changes fastest.
Arguments:
- displacement: float32 [3, 32, 256, 512], P(None, None, 'slab', 'gy'), may hold values from -6 to 6
- previous: float32 [3, 32, 256, 512], P(None, None, 'slab', 'gy'), may hold values from -6 to 6
- shear_coef: float32 [32, 256, 512], P(None, 'slab', 'gy'), may hold values from 0.04 to 0.16
- bulk_coef: float32 [32, 256, 512], P(None, 'slab', 'gy'), may hold values from 0.02 to 0.16
- cell_index: int32 [131072], P(('slab', 'gy')), may hold values from 0 to 131071, as said below
- archetype_id: int32 [131072, 1], P(('slab', 'gy')), may hold values from 0 to 1023; in each aligned block of 1024 rows (0 to 1023, 1024 to 2047, ...) at most 2 rows name the same one
- transition: bfloat16 [1024, 256, 256], P(('slab', 'gy')), may hold values from -1 to 1
- forcing: float32 [1024, 3, 256], P(('slab', 'gy')), may hold values from -3 to 3
Outputs:
- final_field: float32 [3, 32, 256, 512], P(None, None, 'slab', 'gy')
- building_state: float32 [131072, 256], P(('slab', 'gy'))
The draws below stay inside these ranges and needn't reach their ends.
Inputs may be any that keep to these rules, and one draw needn't show every extreme that they name: `cell_index`: building b's cell has x between s * 8 and s * 8 + 7, where s = (b // 1024) // 4; y is any. `archetype_id`: among the 1024 buildings of one device no archetype appears more than 2 times.
All inputs are finite; a program needn't handle non-finite values.
Results may differ from the reference program's by a relative error of at most 0.0023.
Values sent between devices are 32-bit elements; how exact they have to be, the bound alone decides.
No kernel may reach another device: no remote copies, remote signals or barrier semaphores. Data moves between devices by JAX's collectives and lax.ppermute only.
A program may use at most 64 MiB of HBM per device.

```python
import math
import jax
import jax.numpy as jnp
import numpy as np
from jax import lax

NZ = 32
CX = 8
CY = 128
ARCHETYPES = 1024
STATES = 256
BLD_DEV = 1024
COUPLINGS = 4
EVERY = 5
SUB = 6
NX = 256
NY = 512
BUILDINGS = 131072
CAP = 2
DEVICES = 128


def draw_cell_index(key, part):
    rows = jnp.arange(BUILDINGS, dtype=jnp.int32)
    strip = rows // BLD_DEV // (NY // CY)
    key_x, key_y = jax.random.split(jax.random.fold_in(key, 11))
    along_x = jax.random.randint(key_x, (BUILDINGS,), 0, CX, dtype=jnp.int32)
    along_y = jax.random.randint(key_y, (BUILDINGS,), 0, NY, dtype=jnp.int32)
    return ((strip * CX + along_x) * NY + along_y).astype(jnp.int32)


def draw_transition(key, part):
    key_a, key_b = jax.random.split(jax.random.fold_in(key, 7))
    noise = jax.random.normal(key_a, (ARCHETYPES, STATES, STATES), jnp.float32) * (0.2 / math.sqrt(STATES))
    noise = jnp.clip(noise, -0.25, 0.25)
    diagonal = jax.random.uniform(key_b, (ARCHETYPES, STATES), jnp.float32, 0.4, 0.7)
    matrix = noise + diagonal[:, :, None] * jnp.eye(STATES, dtype=jnp.float32)[None]
    return matrix.astype(jnp.bfloat16)


def block_levels(own_key, dims, cuts, smallest, high):
    def one(dim, blocks):
        heights = jax.random.uniform(jax.random.fold_in(jax.random.fold_in(own_key, 6), dim), (blocks,), jnp.float32, smallest / len(cuts), high / len(cuts))
        return jnp.repeat(jnp.exp(heights), dims[dim] // blocks).reshape((-1,) + (1,) * (len(dims) - dim - 1))

    factor_of = one(*cuts[0])
    for cut in cuts[1:]:
        factor_of = factor_of * one(*cut)
    return factor_of


def deal_out(stream_key, own, number, rows, number_of, top, bound, lean):
    sequence = jax.random.permutation(stream_key, number_of)
    crowded, ordinary = load_shares(number_of, rows * top, bound, lean, True), load_shares(number_of, rows * top, bound, lean, False)
    places = jnp.arange(number_of)

    def named(tallies, rotation):
        used = int((tallies > 0).sum())
        fixed = max(1, used // 4)
        moved = fixed + (places - fixed + rotation * (used - fixed)) % max(1, number_of - fixed)
        return jnp.zeros((number_of,), jnp.int32).at[sequence[jnp.where(places < fixed, places, moved)]].set(jnp.asarray(tallies, jnp.int32))

    tallies = jnp.where(number % 4 == 0, named(crowded, number // 4), named(ordinary, number - number // 4 - 1))
    mixed = jax.random.permutation(jax.random.fold_in(own, 3), number_of)
    giver, sink = mixed[0:number_of // 2 * 2:2], mixed[1:number_of // 2 * 2:2]
    room = jnp.minimum(tallies[giver] - 1, bound - tallies[sink]) // 2
    room = jnp.where((giver == sequence[0]) | (sink == sequence[0]) | (tallies[sink] == 0), 0, jnp.maximum(room, 0))
    moved = jax.random.randint(jax.random.fold_in(own, 4), (number_of // 2,), 0, 1 << 20) % (room + 1)
    tallies = tallies.at[giver].add(-moved).at[sink].add(moved)
    items = jnp.searchsorted(jnp.cumsum(tallies), jnp.arange(rows * top), side="right").astype(jnp.int32)
    table = items.reshape(top, rows).T
    table = table[jax.random.permutation(jax.random.fold_in(own, 1), rows)]
    rotation = jax.random.randint(jax.random.fold_in(own, 2), (rows, 1), 0, top)
    return jnp.take_along_axis(table, (jnp.arange(top)[None, :] + rotation) % top, axis=1)


def load_shares(count, total, bound, lean, full):
    portions = [(1 << 20) // math.isqrt(rank ** lean) + 1 for rank in range(1, count + 1)]
    largest = bound if full else min(bound, max(-(-total // count), total * portions[0] // sum(portions)))
    least = 1 if total - largest >= count - 1 else 0
    holding, surplus = [largest] + [least] * (count - 1), total - largest - least * (count - 1)
    while surplus > 0:
        movable = [i for i in range(1, count) if holding[i] < largest] or [i for i in range(1, count) if holding[i] < bound]
        mass, left = sum([portions[i] for i in movable]), surplus
        for i in movable:
            extra = min(bound - holding[i], max(1, left * portions[i] // mass), surplus)
            holding[i] = holding[i] + extra
            surplus = surplus - extra
    return np.array(holding)


def centred(rng, shape, width, bound, cuts=(), held_as=jnp.bfloat16):
    array = jax.random.normal(rng, shape, jnp.float32) * width
    if len(cuts) > 0:
        array = block_levels(rng, shape, cuts, -0.22, 0.18) * array
    return jnp.clip(array, min=-bound, max=bound).astype(held_as)


def setup_inputs(seed: int = 0) -> dict:
    streams_of = jax.random.split(jax.random.key(seed), 9)
    displacement = centred(streams_of[0], (3, NZ, NX, NY), 1.0, 6.0, ((2, 32), (3, 4)), jnp.float32)
    previous = centred(streams_of[1], (3, NZ, NX, NY), 1.0, 6.0, ((2, 32), (3, 4)), jnp.float32)
    shear_coef = jnp.clip(jnp.exp(math.log(0.16) - 1.3862944 * jax.random.uniform(streams_of[2], (NZ, NX, NY), jnp.float32) ** block_levels(streams_of[2], (NZ, NX, NY), ((1, 32), (2, 4)), -0.2, 0.2)), 0.04, 0.16)
    bulk_coef = jnp.clip(jnp.exp(math.log(0.16) - 2.0794415 * jax.random.uniform(streams_of[3], (NZ, NX, NY), jnp.float32) ** block_levels(streams_of[3], (NZ, NX, NY), ((1, 32), (2, 4)), -0.2, 0.2)), 0.02, 0.16)
    cell_index = draw_cell_index(jax.random.fold_in(streams_of[8], 71), 0)
    archetype_id_keys = jax.random.split(jax.random.fold_in(streams_of[5], 1), BUILDINGS // BLD_DEV)
    archetype_id_turns = jax.random.permutation(jax.random.fold_in(streams_of[5], 3), BUILDINGS // BLD_DEV)
    archetype_id = jax.vmap(lambda own, number: deal_out(jax.random.fold_in(streams_of[5], 2), own, number, BLD_DEV, ARCHETYPES, 1, CAP, 2))(archetype_id_keys, archetype_id_turns).reshape((BUILDINGS, 1))
    transition = draw_transition(jax.random.fold_in(streams_of[8], 71), 0)
    forcing = centred(streams_of[7], (ARCHETYPES, 3, STATES), 0.5, 3.0, ((0, 128),), jnp.float32)
    return dict(displacement=displacement, previous=previous, shear_coef=shear_coef, bulk_coef=bulk_coef, cell_index=cell_index, archetype_id=archetype_id, transition=transition, forcing=forcing)


FIRST = ((-2, 1.0 / 12.0), (-1, -8.0 / 12.0), (1, 8.0 / 12.0), (2, -1.0 / 12.0))
SECOND = ((-2, -1.0 / 12.0), (-1, 16.0 / 12.0), (0, -30.0 / 12.0), (1, 16.0 / 12.0), (2, -1.0 / 12.0))
COMPONENT_AXIS = (1, 2, 0)


def pad_depth(padded):
    extent = padded.shape
    below = jnp.zeros((extent[0], 2, extent[2], extent[3]), padded.dtype)
    return jnp.concatenate([padded[:, 2:0:-1], padded, below], axis=1)


def shifted(volume, offsets):
    starts = [2 + offsets[0], 2 + offsets[1], 2 + offsets[2]]
    return volume[starts[0]:starts[0] + volume.shape[0] - 4,
                  starts[1]:starts[1] + volume.shape[1] - 4,
                  starts[2]:starts[2] + volume.shape[2] - 4]


def second_along(volume, main_axis):
    summed = None
    for amount, weight in SECOND:
        offsets = [0, 0, 0]
        offsets[main_axis] = amount
        term = weight * shifted(volume, offsets)
        summed = term if summed is None else summed + term
    return summed


def mixed_along(volume, main_axis, other_axis):
    summed = None
    for amount_a, weight_a in FIRST:
        for amount_b, weight_b in FIRST:
            offsets = [0, 0, 0]
            offsets[main_axis] = amount_a
            offsets[other_axis] = amount_b
            term = (weight_a * weight_b) * shifted(volume, offsets)
            summed = term if summed is None else summed + term
    return summed


def accelerate(padded, shear_coef, bulk_coef):
    results = []
    for component in range(3):
        volume = padded[component]
        main_axis = COMPONENT_AXIS[component]
        seconds = [second_along(volume, axis_a) for axis_a in range(3)]
        laplacian = seconds[0] + seconds[1] + seconds[2]
        divergence = seconds[main_axis]
        for partner in range(3):
            if partner != component:
                divergence = divergence + mixed_along(padded[partner], main_axis, COMPONENT_AXIS[partner])
        results.append(shear_coef * laplacian + bulk_coef * divergence)
    return jnp.stack(results)


def advance_grid(field, former, shear_coef, bulk_coef):
    padded = pad_depth(jnp.pad(field, ((0, 0), (0, 0), (2, 2), (2, 2))))
    return 2.0 * field - former + accelerate(padded, shear_coef, bulk_coef)


def ranks_of(members):
    order = jnp.arange(members.shape[0], dtype=jnp.int32)
    earlier = (members[:, None] == members[None, :]) & (order[None, :] < order[:, None])
    return jnp.sum(earlier.astype(jnp.int32), axis=1).astype(jnp.int32)


def reference(displacement, previous, shear_coef, bulk_coef, cell_index, archetype_id, transition, forcing):
    kinds = archetype_id[:, 0].astype(jnp.int32)
    position = lax.map(ranks_of, kinds.reshape(DEVICES, BLD_DEV)).reshape(-1).astype(jnp.int32)
    home_dev = (jnp.arange(BUILDINGS, dtype=jnp.int32) // BLD_DEV).astype(jnp.int32)
    states = jnp.zeros((BUILDINGS, STATES), jnp.float32)
    matrices = transition.astype(jnp.float32)
    field, former = displacement, previous
    for moment in range(COUPLINGS):
        for inner in range(EVERY):
            field, former = advance_grid(field, former, shear_coef, bulk_coef), field
        surface = field[:, 0].reshape(3, NX * NY)
        ground = jnp.take(surface, cell_index, axis=1)
        slots = jnp.zeros((ARCHETYPES, DEVICES, CAP, STATES), jnp.float32).at[kinds, home_dev, position].set(states)
        motion = jnp.zeros((ARCHETYPES, 3, DEVICES, CAP), jnp.float32).at[kinds, :, home_dev, position].set(ground.T)
        drive = motion[:, 0, :, :, None] * forcing[:, 0, None, None, :]
        drive = drive + motion[:, 1, :, :, None] * forcing[:, 1, None, None, :]
        drive = drive + motion[:, 2, :, :, None] * forcing[:, 2, None, None, :]
        for inner in range(SUB):
            rounded = lax.optimization_barrier(slots.astype(jnp.bfloat16)).astype(jnp.float32)
            slots = jnp.einsum("adck,ajk->adcj", rounded, matrices) + drive
        states = slots[kinds, home_dev, position]
    return field, states
```

```python
import functools

import jax
import jax.numpy as jnp
import numpy as np
from jax import lax
from jax.experimental import pallas as pl
from jax.experimental.pallas import tpu as pltpu
from jax.sharding import PartitionSpec as P

COUPLINGS = 4
EVERY = 5
SUB = 6
NZ = 32
CX = 8
CY = 128
GROUPS = 4
ROWS = CY // GROUPS
STEPS = 4
HALO = 2 * STEPS
X0 = HALO + 2
XE = 2 * X0 + CX
R0 = 16
RE = 64
VMEM = pl.BlockSpec(memory_space=pltpu.VMEM)
SMEM = pl.BlockSpec(memory_space=pltpu.SMEM)


def depth_weights():
    z = np.arange(128) % NZ
    second = np.zeros((5, 128), np.float32)
    first = np.zeros((5, 128), np.float32)
    second[:] = np.array([-1, 16, -30, 16, -1], np.float32)[:, None]
    first[:] = np.array([1, -8, 0, 8, -1], np.float32)[:, None]
    for table in (second, first):
        for lane in range(128):
            for k in range(5):
                source = z[lane] + k - 2
                weight = table[k, lane]
                if source < 0:
                    table[k, lane] = 0.0
                    table[-source - z[lane] + 2, lane] += weight
                elif source >= NZ:
                    table[k, lane] = 0.0
    both = np.concatenate([second, first])
    return np.broadcast_to(both[:, None, :], (10, 8, 128)).copy()


def along_depth(value, weights):
    total = weights[2] * value
    for k, shift in ((0, 2), (1, 1), (3, 127), (4, 126)):
        total = total + weights[k] * pltpu.roll(value, shift, 1)
    return total


def advance(step, field, former, shear, bulk, part_x, part_y, part_z, weights_ref):
    row_a, tiles_a = R0 - HALO - 2 + 2 * step, -(-(ROWS + 2 * HALO + 4 - 4 * step) // 8)
    row_b, tiles_b = R0 - HALO + 2 * step, -(-(ROWS + 2 * HALO - 4 * step) // 8)

    def firsts(x, carry):
        first_z = [weights_ref[5 + k] for k in range(5)]
        for k in range(tiles_a):
            r = row_a + 8 * k
            at = lambda c, dx, dr: field[c, x + dx, pl.ds(r + dr, 8), :]
            along_z = along_depth(at(2, 0, 0), first_z)
            along_y = 8.0 * (at(1, 0, 1) - at(1, 0, -1)) - (at(1, 0, 2) - at(1, 0, -2))
            along_x = 8.0 * (at(0, 1, 0) - at(0, -1, 0)) - (at(0, 2, 0) - at(0, -2, 0))
            part_x[x, pl.ds(r, 8), :] = along_y + along_z
            part_y[x, pl.ds(r, 8), :] = along_x + along_z
            part_z[x, pl.ds(r, 8), :] = along_x + along_y
        return carry

    def update(x, carry):
        second_z = [weights_ref[k] for k in range(5)]
        first_z = [weights_ref[5 + k] for k in range(5)]
        for k in range(tiles_b):
            r = row_b + 8 * k
            rows = pl.ds(r, 8)
            s = shear[x, rows, :]
            b = bulk[x, rows, :]
            for c in range(3):
                at = lambda dx, dr: field[c, x + dx, pl.ds(r + dr, 8), :]
                centre = at(0, 0)
                d_x = 16.0 * (at(1, 0) + at(-1, 0)) - (at(2, 0) + at(-2, 0))
                d_y = 16.0 * (at(0, 1) + at(0, -1)) - (at(0, 2) + at(0, -2))
                d_z = along_depth(centre, second_z)
                if c == 0:
                    own = d_x - 30.0 * centre
                    mixed = 8.0 * (part_x[x + 1, rows, :] - part_x[x - 1, rows, :]) - (
                        part_x[x + 2, rows, :] - part_x[x - 2, rows, :]
                    )
                elif c == 1:
                    own = d_y - 30.0 * centre
                    mixed = 8.0 * (
                        part_y[x, pl.ds(r + 1, 8), :] - part_y[x, pl.ds(r - 1, 8), :]
                    ) - (part_y[x, pl.ds(r + 2, 8), :] - part_y[x, pl.ds(r - 2, 8), :])
                else:
                    own = d_z
                    mixed = along_depth(part_z[x, rows, :], first_z)
                laplacian = (d_x + d_y) + (d_z - 60.0 * centre)
                change = s * laplacian + b * (own + (1.0 / 12.0) * mixed)
                former[c, x, rows, :] = (2.0 * centre - former[c, x, rows, :]) + change
        return carry

    lax.fori_loop(2 * step, XE - 2 * step, firsts, 0)
    lax.fori_loop(2 * step + 2, XE - 2 * step - 2, update, 0)


def place_block(block, low, high, exists, x_from, targets):
    lane = lax.broadcasted_iota(jnp.int32, (8, 128), 1)
    here, from_low, from_high = exists

    def column(x, carry):
        for f, target in enumerate(targets):
            for k in range(ROWS // 8):
                value = jnp.where(here, block[f, x, pl.ds(8 * k, 8), :], 0.0)
                target[x_from + x, pl.ds(R0 + 8 * k, 8), :] = value
            last = jnp.where(here, block[f, x, pl.ds(ROWS - 8, 8), :], 0.0)
            head = jnp.where(here, block[f, x, pl.ds(0, 8), :], 0.0)
            below = jnp.where(from_low, low[f, x, :, :], 0.0)
            above = jnp.where(from_high, high[f, x, :, :], 0.0)
            target[x_from + x, pl.ds(R0 - 8, 8), :] = pltpu.roll(
                jnp.where(lane >= 96, below, last), 32, 1
            )
            target[x_from + x, pl.ds(R0 + ROWS, 8), :] = pltpu.roll(
                jnp.where(lane < 32, above, head), 96, 1
            )
        return carry

    lax.fori_loop(0, CX, column, 0)


def grid_kernel(first, snap_step, edge, weights_ref, *refs):
    blocks = [refs[3 * i : 3 * i + 3] for i in range(3)]
    refs = refs[9:]
    if first:
        out, low_out, high_out, shear, bulk = refs[:5]
        refs = refs[5:]
    else:
        shear, bulk, out, low_out, high_out = refs[:5]
        refs = refs[5:]
    snap = None
    if snap_step is not None:
        snap = refs[0]
        refs = refs[1:]
    fields = refs[:2]
    parts = refs[2:5]

    low_here, high_here = edge[2] == 1, edge[3] == 1
    for i, (block, low, high) in enumerate(blocks):
        here = (None, edge[0] == 1, edge[1] == 1)[i]
        x_from = (X0, X0 - CX, X0 + CX)[i]
        targets = [fields[f // 3].at[f % 3] for f in range(6)]
        if first:
            targets = targets + [shear, bulk]
        if here is None:
            exists = (low_here | high_here | True, low_here, high_here)
        else:
            exists = (
                here,
                jnp.logical_and(here, low_here),
                jnp.logical_and(here, high_here),
            )
        place_block(block, low, high, exists, x_from, targets)

    now, before = fields
    for step in range(1, STEPS + 1):
        advance(step, now, before, shear, bulk, *parts, weights_ref)
        now, before = before, now
        if step == snap_step:
            snap[...] = now[:, pl.ds(X0, CX), pl.ds(R0, ROWS), :]
    for f, source in ((0, now), (3, before)):
        out[pl.ds(f, 3)] = source[:, pl.ds(X0, CX), pl.ds(R0, ROWS), :]
        low_out[pl.ds(f, 3)] = source[:, pl.ds(X0, CX), pl.ds(R0, 8), :]
        high_out[pl.ds(f, 3)] = source[:, pl.ds(X0, CX), pl.ds(R0 + ROWS - 8, 8), :]


def run_grid(first, snap_step, edge, weights, arrays, coefs):
    shape = lambda *s: jax.ShapeDtypeStruct(s, jnp.float32)
    outs = [shape(6, CX, ROWS, 128), shape(6, CX, 8, 128), shape(6, CX, 8, 128)]
    operands = [edge, weights, *arrays]
    if first:
        outs += [shape(XE, RE, 128)] * 2
    else:
        operands += list(coefs)
    if snap_step is not None:
        outs.append(shape(3, CX, ROWS, 128))
    return pl.pallas_call(
        functools.partial(grid_kernel, first, snap_step),
        out_shape=outs,
        in_specs=[SMEM] + [VMEM] * (len(operands) - 1),
        out_specs=[VMEM] * len(outs),
        scratch_shapes=[pltpu.VMEM((3, XE, RE, 128), jnp.float32)] * 2
        + [pltpu.VMEM((XE, RE, 128), jnp.float32)] * 3,
        compiler_params=pltpu.CompilerParams(vmem_limit_bytes=40 << 20),
        cost_estimate=pl.CostEstimate(
            flops=40_000_000, bytes_accessed=8 << 20, transcendentals=0
        ),
        name="grid_steps",
    )(*operands)


def response_kernel(transition, forcing, out, state, total):
    arch = transition.shape[0]
    state[...] = jnp.zeros_like(state)
    out[...] = jnp.zeros_like(out)
    for a in range(arch):
        state[a, 0:3, :] = forcing[a]

    def one(j, carry):
        for a in range(arch):
            now = state[a]
            total[a] = total[a] + now
            high = now.astype(jnp.bfloat16)
            low = (now - high.astype(jnp.float32)).astype(jnp.bfloat16)
            product = lax.dot_general(
                jnp.concatenate([high, low], axis=0),
                transition[a],
                (((1,), (1,)), ((), ())),
                preferred_element_type=jnp.float32,
            )
            state[a] = product[0:8] + product[8:16]
        return carry

    for group in range(COUPLINGS):
        moment = COUPLINGS - 1 - group
        total[...] = jnp.zeros_like(total)
        lax.fori_loop(0, SUB, one, 0)
        for a in range(arch):
            for c in range(3):
                for h in range(2):
                    row = 2 * c + h
                    out[a, moment, row : row + 1, :] = total[
                        a, c : c + 1, 128 * h : 128 * h + 128
                    ]
            if group < COUPLINGS - 1:
                scale = jnp.maximum(jnp.max(jnp.abs(state[a]), keepdims=True), 1.0)
                state[a] = state[a] / scale
                out[a, moment, 6:7, :] = jnp.broadcast_to(scale, (1, 128))


def responses(transition, forcing):
    arch, width = transition.shape[0], transition.shape[1]
    return pl.pallas_call(
        response_kernel,
        out_shape=jax.ShapeDtypeStruct((arch, COUPLINGS, 8, 128), jnp.float32),
        in_specs=[VMEM, VMEM],
        out_specs=VMEM,
        scratch_shapes=[pltpu.VMEM((arch, 8, width), jnp.float32)] * 2,
        compiler_params=pltpu.CompilerParams(vmem_limit_bytes=24 << 20),
        cost_estimate=pl.CostEstimate(
            flops=20_000_000, bytes_accessed=2 << 20, transcendentals=0
        ),
        name="responses",
    )(transition, forcing)


def building_kernel(kinds, place, across, surface, table, out, ground):
    count = out.shape[0]
    cells = surface.shape[0] * CY
    picks = (lax.broadcasted_iota(jnp.int32, (cells, count), 0) == place[...]).astype(jnp.bfloat16)
    values = jnp.concatenate([surface[j] for j in range(surface.shape[0])], axis=1)
    high = values.astype(jnp.bfloat16)
    rest = values - high.astype(jnp.float32)
    low = rest.astype(jnp.bfloat16)
    least = (rest - low.astype(jnp.float32)).astype(jnp.bfloat16)
    picked = jnp.dot(
        jnp.concatenate([high, low, least], axis=0), picks, preferred_element_type=jnp.float32
    )
    n = values.shape[0]
    picked = picked[0:n] + picked[n : 2 * n] + picked[2 * n : 3 * n]
    here = lax.broadcasted_iota(jnp.int32, (CX, count), 0) == across[...]
    row = lax.broadcasted_iota(jnp.int32, (8, count), 0)
    for m in range(COUPLINGS):
        rows = []
        for c in range(3):
            k = 3 * m + c
            value = jnp.where(here, picked[CX * k : CX * k + CX], 0.0)
            rows.append(jnp.sum(value, axis=0, keepdims=True))
        ground[m] = jnp.where(
            row < 2, rows[0], jnp.where(row < 4, rows[1], jnp.where(row < 6, rows[2], 0.0))
        )

    def tile(t, carry):
        base = pl.multiple_of(t * 128, 128)
        motion = [ground[m, :, pl.ds(base, 128)] for m in range(COUPLINGS)]
        slot = lax.broadcasted_iota(jnp.int32, (8, 128), 0)
        for eight in range(16):
            halves = [jnp.zeros((8, 128), jnp.float32)] * 2
            for k in range(8):
                i = 8 * eight + k
                kind = kinds[base + i]
                total = None
                for m in range(COUPLINGS):
                    term = table[kind, m] * jnp.broadcast_to(motion[m][:, i : i + 1], (8, 128))
                    if total is None:
                        total = term
                    else:
                        scale = jnp.broadcast_to(table[kind, m, 6:7, :], (8, 128))
                        total = total * scale + term
                total = total + pltpu.roll(total, 4, 0)
                total = total + pltpu.roll(total, 2, 0)
                other = pltpu.roll(total, 1, 0)
                pair = (total, other) if k % 2 == 0 else (other, total)
                halves = [jnp.where(slot == k, new, old) for new, old in zip(pair, halves)]
            rows = pl.ds(base + 8 * eight, 8)
            out[rows, 0:128] = halves[0]
            out[rows, 128:256] = halves[1]
        return carry

    lax.fori_loop(0, count // 128, tile, 0)


def building_states(kinds, place, across, surface, table, width):
    count = kinds.shape[0]
    return pl.pallas_call(
        building_kernel,
        out_shape=jax.ShapeDtypeStruct((count, width), jnp.float32),
        in_specs=[SMEM] + [VMEM] * 4,
        out_specs=VMEM,
        scratch_shapes=[pltpu.VMEM((COUPLINGS, 8, count), jnp.float32)],
        compiler_params=pltpu.CompilerParams(vmem_limit_bytes=50 << 20),
        cost_estimate=pl.CostEstimate(
            flops=20_000_000, bytes_accessed=18 << 20, transcendentals=0
        ),
        name="buildings",
    )(kinds, place[None, :], across[None, :], surface, table)


def ring(value, axis, shift):
    count = lax.axis_size(axis)
    return lax.ppermute(value, axis, [(i, (i + shift) % count) for i in range(count)])


def exchange(own, top, bottom):
    low, high = ring(bottom, "gy", 1), ring(top, "gy", -1)
    arrays = [own, low, high]
    for shift in (1, -1):
        arrays += [ring(own, "slab", shift)]
        arrays += [ring(low, "slab", shift), ring(high, "slab", shift)]
    return arrays


def per_device(
    displacement, previous, shear_coef, bulk_coef, cell_index, archetype_id, transition, forcing
):
    width = transition.shape[1]
    slab, gy = lax.axis_index("slab"), lax.axis_index("gy")
    slabs, strips = lax.axis_size("slab"), lax.axis_size("gy")
    edge = jnp.stack([slab > 0, slab < slabs - 1, gy > 0, gy < strips - 1]).astype(jnp.int32)
    weights = jnp.asarray(depth_weights())

    stacked = jnp.concatenate(
        [displacement, previous, shear_coef[None] / 12.0, bulk_coef[None] / 12.0]
    )
    own = stacked.reshape(8, NZ, CX, GROUPS, ROWS).transpose(0, 2, 4, 3, 1)
    own = own.reshape(8, CX, ROWS, 128)
    arrays = exchange(own, own[:, :, :8], own[:, :, ROWS - 8 :])

    table = lax.all_gather(responses(transition, forcing), ("slab", "gy"), axis=0, tiled=True)

    snaps = []
    coefs = None
    blocks = COUPLINGS * EVERY // STEPS
    for block in range(blocks):
        snap_step = next(
            (s for s in range(1, STEPS + 1) if (block * STEPS + s) % EVERY == 0), None
        )
        result = run_grid(block == 0, snap_step, edge, weights, arrays, coefs)
        own, top, bottom = result[:3]
        if block == 0:
            coefs = result[3:5]
        if snap_step is not None:
            ground = result[-1][..., ::NZ]
            snaps.append(ground.transpose(0, 1, 3, 2).reshape(3 * CX, CY))
        if block < blocks - 1:
            arrays = exchange(own, top, bottom)
    final = own[:3].reshape(3, CX, ROWS, GROUPS, NZ).transpose(0, 4, 1, 3, 2)
    final = final.reshape(3, NZ, CX, CY)

    mine = jnp.concatenate(snaps)
    surface = jnp.stack([mine] + [ring(mine, "gy", shift) for shift in range(1, strips)])
    columns = strips * CY
    along_y = cell_index % columns
    across = cell_index // columns - slab * CX
    place = (gy - along_y // CY) % strips * CY + along_y % CY
    states = building_states(archetype_id[:, 0], place, across, surface, table, width)
    return (final, states)


def solution(mesh):
    in_specs = (
        P(None, None, "slab", "gy"),
        P(None, None, "slab", "gy"),
        P(None, "slab", "gy"),
        P(None, "slab", "gy"),
        P(("slab", "gy")),
        P(("slab", "gy"), None),
        P(("slab", "gy"), None, None),
        P(("slab", "gy"), None, None),
    )
    out_specs = (P(None, None, "slab", "gy"), P(("slab", "gy"), None))
    return jax.shard_map(
        per_device, mesh=mesh, in_specs=in_specs, out_specs=out_specs, check_vma=False
    )
```

```python
import functools

import jax
import jax.numpy as jnp
import numpy as np
from jax import lax
from jax.experimental import pallas as pl
from jax.experimental.pallas import tpu as pltpu
from jax.sharding import PartitionSpec as P

COUPLINGS = 4
EVERY = 5
SUB = 6
NZ = 32
CX = 8
CY = 128
GROUPS = 4
ROWS = CY // GROUPS
STEPS = 4
X0 = 2 * STEPS + 2
XE = 2 * X0 + CX
TILES_Y = (2, 1, 2, 1, 1)
R0 = 8 * max(TILES_Y) + 8
RE = 2 * R0 + ROWS
CHUNK = 4
VMEM = pl.BlockSpec(memory_space=pltpu.VMEM)
SMEM = pl.BlockSpec(memory_space=pltpu.SMEM)


def depth_weights():
    matrix = np.zeros((128, 256), np.float32)
    for lane in range(128):
        base, z = lane // NZ * NZ, lane % NZ
        for k, offset in enumerate(range(-2, 3)):
            source = abs(z + offset)
            if source < NZ:
                matrix[base + source, lane] += (-1, 16, -30, 16, -1)[k]
                matrix[base + source, 128 + lane] += (1, -8, 0, 8, -1)[k]
    return np.concatenate([matrix, matrix])


def block_of_lanes(shape):
    return lax.broadcasted_iota(jnp.int32, shape, len(shape) - 1) // NZ


def turn(value, blocks):
    shift = NZ * (blocks % GROUPS)
    return pltpu.roll(value, shift, 1) if shift else value


def pick_block(values, j):
    lanes = block_of_lanes(values[0].shape)
    result = turn(values[0], 0 - j)
    for i in range(1, GROUPS):
        result = jnp.where(lanes == i, turn(values[i], i - j), result)
    return result


def advance(step, tiles_y, field, former, shear, bulk, scratch, weights_ref):
    second_z, part_x, part_y, first_zx, first_zy = scratch
    halo = 8 * tiles_y
    row_a, tiles_a = R0 - halo - 2 + 2 * step, -(-(ROWS + 2 * halo + 4 - 4 * step) // 8)
    row_b, tiles_b = R0 - halo + 2 * step, -(-(ROWS + 2 * halo - 4 * step) // 8)
    start_a, count_a = 2 * step, XE - 4 * step
    start_b, count_b = start_a + 2, count_a - 4
    height = 8 * tiles_a
    window = pl.ds(row_a, height)

    def firsts(chunk, carry):
        x = start_a + CHUNK * chunk
        values = jnp.concatenate(
            [field[c, x + i, window, :] for c in range(3) for i in range(CHUNK)]
        )
        high = values.astype(jnp.bfloat16)
        low = (values - high.astype(jnp.float32)).astype(jnp.bfloat16)
        along_z = jnp.dot(
            jnp.concatenate([high, low], axis=1),
            weights_ref[...],
            preferred_element_type=jnp.float32,
        )
        for i in range(CHUNK):
            for c in range(3):
                at = (CHUNK * c + i) * height
                second_z[c, x + i, window, :] = along_z[at : at + height, 0:128]
            at = i * height
            first_zx[x + i, window, :] = along_z[at : at + height, 128:256]
            at = (CHUNK + i) * height
            first_zy[x + i, window, :] = along_z[at : at + height, 128:256]
        for k in range(tiles_a):
            r = row_a + 8 * k
            rows = pl.ds(r, 8)
            across = [field[0, x + d, rows, :] for d in range(-2, CHUNK + 2)]
            for i in range(CHUNK):
                at = lambda d: field[1, x + i, pl.ds(r + d, 8), :]
                first_y = 8.0 * (at(1) - at(-1)) - (at(2) - at(-2))
                first_x = 8.0 * (across[i + 3] - across[i + 1]) - (across[i + 4] - across[i])
                place = (2 * CHUNK + i) * height + 8 * k
                first_z = along_z[place : place + 8, 128:256]
                part_x[x + i, rows, :] = first_y + first_z
                part_y[x + i, rows, :] = first_x + first_z
        return carry

    def update(chunk, carry):
        x = start_b + CHUNK * chunk
        for k in range(tiles_b):
            r = row_b + 8 * k
            rows = pl.ds(r, 8)

            def first_x(ref):
                across = [ref[x + d, rows, :] for d in range(-2, CHUNK + 2)]
                return [
                    8.0 * (across[i + 3] - across[i + 1]) - (across[i + 4] - across[i])
                    for i in range(CHUNK)
                ]

            def first_y(ref, i):
                at = lambda d: ref[x + i, pl.ds(r + d, 8), :]
                return 8.0 * (at(1) - at(-1)) - (at(2) - at(-2))

            for c in range(3):
                across = [field[c, x + d, rows, :] for d in range(-2, CHUNK + 2)]
                if c == 0:
                    mixed = first_x(part_x)
                elif c == 1:
                    mixed = [first_y(part_y, i) for i in range(CHUNK)]
                else:
                    mixed = [
                        value + first_y(first_zy, i)
                        for i, value in enumerate(first_x(first_zx))
                    ]
                for i in range(CHUNK):
                    at = lambda d: field[c, x + i, pl.ds(r + d, 8), :]
                    centre = across[i + 2]
                    d_x = 16.0 * (across[i + 3] + across[i + 1]) - (across[i + 4] + across[i])
                    d_y = 16.0 * (at(1) + at(-1)) - (at(2) + at(-2))
                    d_z = second_z[c, x + i, rows, :]
                    own = (d_x - 30.0 * centre, d_y - 30.0 * centre, d_z)[c]
                    laplacian = (d_x + d_y) + (d_z - 60.0 * centre)
                    change = shear[x + i, rows, :] * laplacian + bulk[x + i, rows, :] * (
                        own + (1.0 / 12.0) * mixed[i]
                    )
                    former[c, x + i, rows, :] = (
                        2.0 * centre - former[c, x + i, rows, :]
                    ) + change
        return carry

    lax.fori_loop(0, count_a // CHUNK, firsts, 0)
    lax.fori_loop(0, count_b // CHUNK, update, 0)


def place_block(own, halo, halo_from, tiles_y, exists, x_from, targets):
    lanes = block_of_lanes((8, 128))
    here, from_low, from_high = exists

    def keep(flag, value):
        return value if flag is None else jnp.where(flag, value, 0.0)

    def columns(q, carry):
        for f, target in enumerate(targets):
            low, high = [
                [
                    keep(
                        (from_low, from_high)[side],
                        halo[
                            f,
                            pl.ds(
                                pl.multiple_of(
                                    halo_from + 8 * ((2 * side + q) * tiles_y + j), 8
                                ),
                                8,
                            ),
                            :,
                        ],
                    )
                    for j in range(tiles_y)
                ]
                for side in range(2)
            ]
            for i in range(4):
                x = 4 * q + i
                first = pl.multiple_of(ROWS * x, 8)
                tiles = [
                    keep(here, own[f, pl.ds(first + 8 * k, 8), :]) for k in range(ROWS // 8)
                ]
                for k in range(ROWS // 8):
                    target[x_from + x, pl.ds(R0 + 8 * k, 8), :] = tiles[k]
                for j in range(tiles_y):
                    target[x_from + x, pl.ds(R0 + 8 * (j - tiles_y), 8), :] = jnp.where(
                        lanes == 0,
                        turn(low[j], 0 - i),
                        turn(tiles[ROWS // 8 - tiles_y + j], 1),
                    )
                    target[x_from + x, pl.ds(R0 + ROWS + 8 * j, 8), :] = jnp.where(
                        lanes == GROUPS - 1,
                        turn(high[j], GROUPS - 1 - i),
                        turn(tiles[j], GROUPS - 1),
                    )
        return carry

    lax.fori_loop(0, CX // 4, columns, 0)


def grid_kernel(block, merged, snap_step, edge, weights_ref, *refs):
    first, last = block == 0, block == len(TILES_Y) - 1
    tiles_y = TILES_Y[block]
    refs = list(refs)
    take = lambda n: [refs.pop(0) for _ in range(n)]
    blocks = [take(1 if merged else 2) for _ in range(3)]
    if first:
        sends = take(1 if TILES_Y[1] < tiles_y else 3)
        shear, bulk = take(2)
    else:
        shear, bulk = take(2)
        sends = take(1) if last or TILES_Y[block + 1] < tiles_y else take(3)
    snap = take(1)[0] if snap_step is not None else None
    fields = take(2)

    low_here, high_here = edge[2] == 1, edge[3] == 1
    for i, arrays in enumerate(blocks):
        here = (None, edge[0] == 1, edge[1] == 1)[i]
        sides = [
            side if here is None else jnp.logical_and(here, side)
            for side in (low_here, high_here)
        ]
        targets = [fields[f // 3].at[f % 3] for f in range(6)]
        if first:
            targets = targets + [shear, bulk]
        place_block(
            arrays[0],
            arrays[-1],
            CX * ROWS if merged else 0,
            tiles_y,
            (here, *sides),
            (X0, X0 - CX, X0 + CX)[i],
            targets,
        )

    now, before = fields
    for step in range(1, STEPS + 1):
        advance(step, tiles_y, now, before, shear, bulk, refs, weights_ref)
        now, before = before, now
        if step == snap_step and not last:
            for x in range(CX):
                snap[:, pl.ds(ROWS * x, ROWS), :] = now[:, X0 + x, pl.ds(R0, ROWS), :]
    if last:
        whole = sends[0]
        for c in range(3):
            for q in range(CX // 4):
                columns = [now[c, X0 + 4 * q + i, pl.ds(R0, ROWS), :] for i in range(4)]
                grid = jnp.concatenate([pick_block(columns, g) for g in range(GROUPS)]).T
                for i in range(4):
                    x = 4 * q + i
                    rows = grid[NZ * i : NZ * i + NZ]
                    whole[pl.ds(c * NZ * CX + x, NZ, stride=CX), :] = rows
                    snap[CX * c + x : CX * c + x + 1, :] = rows[0:1]
        return
    for f in range(6):
        source = (now, before)[f // 3].at[f % 3]
        for x in range(CX):
            sends[0][f, pl.ds(ROWS * x, ROWS), :] = source[X0 + x, pl.ds(R0, ROWS), :]
        if len(sends) == 1:
            depth, far = tiles_y - 1, sends[0]
            spots = ((R0 - 8 * depth, 0), (R0 + ROWS, GROUPS - 1))
            starts = (CX * ROWS, CX * ROWS + 16 * depth)
            outs = (far, far)
        else:
            depth = TILES_Y[block + 1]
            spots = ((R0 + ROWS - 8 * depth, GROUPS - 1), (R0, 0))
            starts, outs = (0, 0), sends[1:]
        for (row, group), start, out in zip(spots, starts, outs):
            for q in range(CX // 4):
                columns = [source[X0 + 4 * q + i, pl.ds(row, 8 * depth), :] for i in range(4)]
                out[f, pl.ds(start + 8 * depth * q, 8 * depth), :] = pick_block(columns, group)


def run_grid(block, snap_step, edge, weights, blocks, coefs):
    shape = lambda *s: jax.ShapeDtypeStruct(s, jnp.float32)
    last = block == len(TILES_Y) - 1
    merged = len(blocks[0]) == 1
    if last:
        outs = [shape(3 * NZ * CX, CY)]
    elif TILES_Y[block + 1] < TILES_Y[block]:
        outs = [shape(6, CX * ROWS + 32 * (TILES_Y[block] - 1), 128)]
    else:
        outs = [shape(6, CX * ROWS, 128)] + [shape(6, 16 * TILES_Y[block + 1], 128)] * 2
    operands = [edge, weights] + [array for arrays in blocks for array in arrays]
    if block == 0:
        outs += [shape(XE, RE, 128)] * 2
    else:
        operands += list(coefs)
    if snap_step is not None:
        outs.append(shape(3 * CX, CY) if last else shape(3, CX * ROWS, 128))
    field = pltpu.VMEM((3, XE, RE, 128), jnp.float32)
    plane = pltpu.VMEM((XE, RE, 128), jnp.float32)
    return pl.pallas_call(
        functools.partial(grid_kernel, block, merged, snap_step),
        out_shape=outs,
        in_specs=[SMEM] + [VMEM] * (len(operands) - 1),
        out_specs=[VMEM] * len(outs),
        scratch_shapes=[field, field, field, plane, plane, plane, plane],
        compiler_params=pltpu.CompilerParams(vmem_limit_bytes=48 << 20),
        cost_estimate=pl.CostEstimate(
            flops=40_000_000, bytes_accessed=8 << 20, transcendentals=0
        ),
        name="grid_steps",
    )(*operands)


def arrange_kernel(now, before, shear, bulk, own, low, high):
    depth = 8 * TILES_Y[0]
    for f in range(8):
        ref, base = ((now, 256 * f), (before, 256 * (f - 3)), (shear, 0), (bulk, 0))[
            f // 3 if f < 6 else f - 4
        ]
        for q in range(CX // 4):
            values = [ref[pl.ds(base + 4 * q + i, NZ, stride=CX), :] for i in range(4)]
            grid = jnp.concatenate(values).T
            if f >= 6:
                grid = grid * (1.0 / 12.0)
            low[f, pl.ds(depth * q, depth), :] = grid[CY - depth : CY]
            high[f, pl.ds(depth * q, depth), :] = grid[0:depth]
            groups = [grid[ROWS * g : ROWS * g + ROWS] for g in range(GROUPS)]
            for i in range(4):
                own[f, pl.ds(ROWS * (4 * q + i), ROWS), :] = pick_block(groups, i)


def arrange(displacement, previous, shear_coef, bulk_coef):
    shape = lambda *s: jax.ShapeDtypeStruct(s, jnp.float32)
    side = shape(8, 16 * TILES_Y[0], 128)
    flat = [a.reshape(-1, CY) for a in (displacement, previous, shear_coef, bulk_coef)]
    return pl.pallas_call(
        arrange_kernel,
        out_shape=[shape(8, CX * ROWS, 128), side, side],
        in_specs=[VMEM] * 4,
        out_specs=[VMEM] * 3,
        compiler_params=pltpu.CompilerParams(vmem_limit_bytes=24 << 20),
        cost_estimate=pl.CostEstimate(
            flops=1_000_000, bytes_accessed=4 << 20, transcendentals=0
        ),
        name="arrange",
    )(*flat)


def response_kernel(transition, forcing, out, state, total):
    arch = transition.shape[0]
    state[...] = jnp.zeros_like(state)
    out[...] = jnp.zeros_like(out)
    for a in range(arch):
        state[a, 0:3, :] = forcing[a]

    def one(j, carry):
        for a in range(arch):
            now = state[a]
            total[a] = total[a] + now
            high = now.astype(jnp.bfloat16)
            low = (now - high.astype(jnp.float32)).astype(jnp.bfloat16)
            product = lax.dot_general(
                jnp.concatenate([high, low], axis=0),
                transition[a],
                (((1,), (1,)), ((), ())),
                preferred_element_type=jnp.float32,
            )
            state[a] = product[0:8] + product[8:16]
        return carry

    for group in range(COUPLINGS):
        moment = COUPLINGS - 1 - group
        total[...] = jnp.zeros_like(total)
        lax.fori_loop(0, SUB, one, 0)
        for a in range(arch):
            for c in range(3):
                for h in range(2):
                    row = 2 * c + h
                    out[a, moment, row : row + 1, :] = total[
                        a, c : c + 1, 128 * h : 128 * h + 128
                    ]
            if group < COUPLINGS - 1:
                scale = jnp.maximum(jnp.max(jnp.abs(state[a]), keepdims=True), 1.0)
                state[a] = state[a] / scale
                out[a, moment, 6:7, :] = jnp.broadcast_to(scale, (1, 128))


def responses(transition, forcing):
    arch, width = transition.shape[0], transition.shape[1]
    return pl.pallas_call(
        response_kernel,
        out_shape=jax.ShapeDtypeStruct((arch, COUPLINGS, 8, 128), jnp.float32),
        in_specs=[VMEM, VMEM],
        out_specs=VMEM,
        scratch_shapes=[pltpu.VMEM((arch, 8, width), jnp.float32)] * 2,
        compiler_params=pltpu.CompilerParams(vmem_limit_bytes=24 << 20),
        cost_estimate=pl.CostEstimate(
            flops=20_000_000, bytes_accessed=2 << 20, transcendentals=0
        ),
        name="responses",
    )(transition, forcing)


def building_kernel(kinds, place, across, surface, table, out, ground):
    count = out.shape[0]
    cells = surface.shape[0] * CY
    picks = (lax.broadcasted_iota(jnp.int32, (cells, count), 0) == place[...]).astype(jnp.bfloat16)
    values = jnp.concatenate([surface[j] for j in range(surface.shape[0])], axis=1)
    high = values.astype(jnp.bfloat16)
    rest = values - high.astype(jnp.float32)
    low = rest.astype(jnp.bfloat16)
    least = (rest - low.astype(jnp.float32)).astype(jnp.bfloat16)
    picked = jnp.dot(
        jnp.concatenate([high, low, least], axis=0), picks, preferred_element_type=jnp.float32
    )
    n = values.shape[0]
    picked = picked[0:n] + picked[n : 2 * n] + picked[2 * n : 3 * n]
    here = lax.broadcasted_iota(jnp.int32, (CX, count), 0) == across[...]
    row = lax.broadcasted_iota(jnp.int32, (8, count), 0)
    for m in range(COUPLINGS):
        rows = []
        for c in range(3):
            k = 3 * m + c
            value = jnp.where(here, picked[CX * k : CX * k + CX], 0.0)
            rows.append(jnp.sum(value, axis=0, keepdims=True))
        ground[m] = jnp.where(
            row < 2, rows[0], jnp.where(row < 4, rows[1], jnp.where(row < 6, rows[2], 0.0))
        )

    def tile(t, carry):
        base = pl.multiple_of(t * 128, 128)
        motion = [ground[m, :, pl.ds(base, 128)] for m in range(COUPLINGS)]
        slot = lax.broadcasted_iota(jnp.int32, (8, 128), 0)
        for eight in range(16):
            halves = [jnp.zeros((8, 128), jnp.float32)] * 2
            for k in range(8):
                i = 8 * eight + k
                kind = kinds[base + i]
                total = None
                for m in range(COUPLINGS):
                    term = table[kind, m] * jnp.broadcast_to(motion[m][:, i : i + 1], (8, 128))
                    if total is None:
                        total = term
                    else:
                        scale = jnp.broadcast_to(table[kind, m, 6:7, :], (8, 128))
                        total = total * scale + term
                total = total + pltpu.roll(total, 4, 0)
                total = total + pltpu.roll(total, 2, 0)
                other = pltpu.roll(total, 1, 0)
                pair = (total, other) if k % 2 == 0 else (other, total)
                halves = [jnp.where(slot == k, new, old) for new, old in zip(pair, halves)]
            rows = pl.ds(base + 8 * eight, 8)
            out[rows, 0:128] = halves[0]
            out[rows, 128:256] = halves[1]
        return carry

    lax.fori_loop(0, count // 128, tile, 0)


def building_states(kinds, place, across, surface, table, width):
    count = kinds.shape[0]
    return pl.pallas_call(
        building_kernel,
        out_shape=jax.ShapeDtypeStruct((count, width), jnp.float32),
        in_specs=[SMEM] + [VMEM] * 4,
        out_specs=VMEM,
        scratch_shapes=[pltpu.VMEM((COUPLINGS, 8, count), jnp.float32)],
        compiler_params=pltpu.CompilerParams(vmem_limit_bytes=50 << 20),
        cost_estimate=pl.CostEstimate(
            flops=20_000_000, bytes_accessed=18 << 20, transcendentals=0
        ),
        name="buildings",
    )(kinds, place[None, :], across[None, :], surface, table)


def ring(value, axis, shift):
    count = lax.axis_size(axis)
    return lax.ppermute(value, axis, [(i, (i + shift) % count) for i in range(count)])


def exchange(own, low=None, high=None):
    if low is None:
        return [[own]] + [[ring(own, "slab", shift)] for shift in (1, -1)]
    sides = jnp.concatenate([ring(low, "gy", 1), ring(high, "gy", -1)], axis=1)
    return [[own, sides]] + [
        [ring(own, "slab", shift), ring(sides, "slab", shift)] for shift in (1, -1)
    ]


def per_device(
    displacement, previous, shear_coef, bulk_coef, cell_index, archetype_id, transition, forcing
):
    width = transition.shape[1]
    slab, gy = lax.axis_index("slab"), lax.axis_index("gy")
    slabs, strips = lax.axis_size("slab"), lax.axis_size("gy")
    edge = jnp.stack([slab > 0, slab < slabs - 1, gy > 0, gy < strips - 1]).astype(jnp.int32)
    weights = jnp.asarray(depth_weights(), jnp.bfloat16)

    blocks = exchange(*arrange(displacement, previous, shear_coef, bulk_coef))
    table = lax.all_gather(responses(transition, forcing), ("slab", "gy"), axis=0, tiled=True)

    snaps = []
    coefs = None
    count = len(TILES_Y)
    for block in range(count):
        snap_step = next(
            (s for s in range(1, STEPS + 1) if (block * STEPS + s) % EVERY == 0), None
        )
        result = run_grid(block, snap_step, edge, weights, blocks, coefs)
        sends = 3 if block < count - 1 and TILES_Y[block + 1] >= TILES_Y[block] else 1
        if block == 0:
            coefs = result[sends : sends + 2]
        if block == count - 1:
            final = result[0].reshape(3, NZ, CX, CY)
            snaps.append(result[1])
        else:
            blocks = exchange(*result[:sends])
            if snap_step is not None:
                ground = result[-1].reshape(3, CX, ROWS, 128)[..., ::NZ]
                snaps.append(ground.transpose(0, 1, 3, 2).reshape(3 * CX, CY))

    mine = jnp.concatenate(snaps)
    surface = jnp.stack([mine] + [ring(mine, "gy", shift) for shift in range(1, strips)])
    columns = strips * CY
    along_y = cell_index % columns
    across = cell_index // columns - slab * CX
    place = (gy - along_y // CY) % strips * CY + along_y % CY
    states = building_states(archetype_id[:, 0], place, across, surface, table, width)
    return (final, states)


def solution(mesh):
    in_specs = (
        P(None, None, "slab", "gy"),
        P(None, None, "slab", "gy"),
        P(None, "slab", "gy"),
        P(None, "slab", "gy"),
        P(("slab", "gy")),
        P(("slab", "gy"), None),
        P(("slab", "gy"), None, None),
        P(("slab", "gy"), None, None),
    )
    out_specs = (P(None, None, "slab", "gy"), P(("slab", "gy"), None))
    return jax.shard_map(
        per_device, mesh=mesh, in_specs=in_specs, out_specs=out_specs, check_vma=False
    )
```

```python
import functools

import jax
import jax.numpy as jnp
import numpy as np
from jax import lax
from jax.experimental import pallas as pl
from jax.experimental.pallas import tpu as pltpu
from jax.sharding import PartitionSpec as P

COUPLINGS = 4
EVERY = 5
SUB = 6
NZ = 32
CX = 8
CY = 128
GROUPS = 4
ROWS = CY // GROUPS
STEPS = 4
X0 = 2 * STEPS + 2
XE = 2 * X0 + CX
TILES_Y = (2, 1, 2, 1, 1)
R0 = 8 * max(TILES_Y) + 8
RE = 2 * R0 + ROWS
CHUNK = 4
SCALES = (2.0**64, 2.0**32, 1.0, 1.0)
VMEM = pl.BlockSpec(memory_space=pltpu.VMEM)
SMEM = pl.BlockSpec(memory_space=pltpu.SMEM)
HBM = pl.BlockSpec(memory_space=pltpu.HBM)


def depth_weights():
    matrix = np.zeros((128, 256), np.float32)
    for lane in range(128):
        base, z = lane // NZ * NZ, lane % NZ
        for k, offset in enumerate(range(-2, 3)):
            source = abs(z + offset)
            if source < NZ:
                matrix[base + source, lane] += (-1, 16, -30, 16, -1)[k]
                matrix[base + source, 128 + lane] += (1, -8, 0, 8, -1)[k]
    return np.concatenate([matrix, matrix])


def block_of_lanes(shape):
    return lax.broadcasted_iota(jnp.int32, shape, len(shape) - 1) // NZ


def turn(value, blocks):
    shift = NZ * (blocks % GROUPS)
    return pltpu.roll(value, shift, 1) if shift else value


def pick_block(values, j):
    lanes = block_of_lanes(values[0].shape)
    result = turn(values[0], 0 - j)
    for i in range(1, GROUPS):
        result = jnp.where(lanes == i, turn(values[i], i - j), result)
    return result


def advance(step, tiles_y, field, former, shear, bulk, scratch, weights_ref):
    second_z, part_x, part_y, first_zx, first_zy = scratch
    halo = 8 * tiles_y
    row_a, tiles_a = R0 - halo - 2 + 2 * step, -(-(ROWS + 2 * halo + 4 - 4 * step) // 8)
    row_b, tiles_b = R0 - halo + 2 * step, -(-(ROWS + 2 * halo - 4 * step) // 8)
    start_a, count_a = 2 * step, XE - 4 * step
    start_b, count_b = start_a + 2, count_a - 4
    height = 8 * tiles_a
    window = pl.ds(row_a, height)

    def firsts(chunk, carry):
        x = start_a + CHUNK * chunk
        values = jnp.concatenate(
            [field[c, x + i, window, :] for c in range(3) for i in range(CHUNK)]
        )
        high = values.astype(jnp.bfloat16)
        low = (values - high.astype(jnp.float32)).astype(jnp.bfloat16)
        along_z = jnp.dot(
            jnp.concatenate([high, low], axis=1),
            weights_ref[...],
            preferred_element_type=jnp.float32,
        )
        for i in range(CHUNK):
            for c in range(3):
                at = (CHUNK * c + i) * height
                second_z[c, x + i, window, :] = along_z[at : at + height, 0:128]
            at = i * height
            first_zx[x + i, window, :] = along_z[at : at + height, 128:256]
            at = (CHUNK + i) * height
            first_zy[x + i, window, :] = along_z[at : at + height, 128:256]
        for k in range(tiles_a):
            r = row_a + 8 * k
            rows = pl.ds(r, 8)
            across = [field[0, x + d, rows, :] for d in range(-2, CHUNK + 2)]
            for i in range(CHUNK):
                at = lambda d: field[1, x + i, pl.ds(r + d, 8), :]
                first_y = 8.0 * (at(1) - at(-1)) - (at(2) - at(-2))
                first_x = 8.0 * (across[i + 3] - across[i + 1]) - (across[i + 4] - across[i])
                place = (2 * CHUNK + i) * height + 8 * k
                first_z = along_z[place : place + 8, 128:256]
                part_x[x + i, rows, :] = first_y + first_z
                part_y[x + i, rows, :] = first_x + first_z
        return carry

    def update(chunk, carry):
        x = start_b + CHUNK * chunk
        for k in range(tiles_b):
            r = row_b + 8 * k
            rows = pl.ds(r, 8)

            def first_x(ref):
                across = [ref[x + d, rows, :] for d in range(-2, CHUNK + 2)]
                return [
                    8.0 * (across[i + 3] - across[i + 1]) - (across[i + 4] - across[i])
                    for i in range(CHUNK)
                ]

            def first_y(ref, i):
                at = lambda d: ref[x + i, pl.ds(r + d, 8), :]
                return 8.0 * (at(1) - at(-1)) - (at(2) - at(-2))

            for c in range(3):
                across = [field[c, x + d, rows, :] for d in range(-2, CHUNK + 2)]
                if c == 0:
                    mixed = first_x(part_x)
                elif c == 1:
                    mixed = [first_y(part_y, i) for i in range(CHUNK)]
                else:
                    mixed = [
                        value + first_y(first_zy, i)
                        for i, value in enumerate(first_x(first_zx))
                    ]
                for i in range(CHUNK):
                    at = lambda d: field[c, x + i, pl.ds(r + d, 8), :]
                    centre = across[i + 2]
                    d_x = 16.0 * (across[i + 3] + across[i + 1]) - (across[i + 4] + across[i])
                    d_y = 16.0 * (at(1) + at(-1)) - (at(2) + at(-2))
                    d_z = second_z[c, x + i, rows, :]
                    own = (d_x - 30.0 * centre, d_y - 30.0 * centre, d_z)[c]
                    laplacian = (d_x + d_y) + (d_z - 60.0 * centre)
                    change = shear[x + i, rows, :] * laplacian + bulk[x + i, rows, :] * (
                        own + (1.0 / 12.0) * mixed[i]
                    )
                    former[c, x + i, rows, :] = (
                        2.0 * centre - former[c, x + i, rows, :]
                    ) + change
        return carry

    lax.fori_loop(0, count_a // CHUNK, firsts, 0)
    lax.fori_loop(0, count_b // CHUNK, update, 0)


def place_block(own, halo, halo_from, tiles_y, exists, x_from, targets):
    lanes = block_of_lanes((8, 128))
    here, from_low, from_high = exists

    def keep(flag, value):
        return value if flag is None else jnp.where(flag, value, 0.0)

    def columns(q, carry):
        for f, target in enumerate(targets):
            low, high = [
                [
                    keep(
                        (from_low, from_high)[side],
                        halo[
                            f,
                            pl.ds(
                                pl.multiple_of(
                                    halo_from + 8 * ((2 * side + q) * tiles_y + j), 8
                                ),
                                8,
                            ),
                            :,
                        ],
                    )
                    for j in range(tiles_y)
                ]
                for side in range(2)
            ]
            for i in range(4):
                x = 4 * q + i
                first = pl.multiple_of(ROWS * x, 8)
                tiles = [
                    keep(here, own[f, pl.ds(first + 8 * k, 8), :]) for k in range(ROWS // 8)
                ]
                for k in range(ROWS // 8):
                    target[x_from + x, pl.ds(R0 + 8 * k, 8), :] = tiles[k]
                for j in range(tiles_y):
                    target[x_from + x, pl.ds(R0 + 8 * (j - tiles_y), 8), :] = jnp.where(
                        lanes == 0,
                        turn(low[j], 0 - i),
                        turn(tiles[ROWS // 8 - tiles_y + j], 1),
                    )
                    target[x_from + x, pl.ds(R0 + ROWS + 8 * j, 8), :] = jnp.where(
                        lanes == GROUPS - 1,
                        turn(high[j], GROUPS - 1 - i),
                        turn(tiles[j], GROUPS - 1),
                    )
        return carry

    lax.fori_loop(0, CX // 4, columns, 0)


def surface_of(field, snap):
    count = 3 * CX
    depth = lax.broadcasted_iota(jnp.int32, (ROWS, 128), 1) % NZ
    gathered = field[0, X0, pl.ds(R0, ROWS), :]
    for k in range(1, count):
        layer = pltpu.roll(field[k // CX, X0 + k % CX, pl.ds(R0, ROWS), :], k, 1)
        gathered = jnp.where(depth == k, layer, gathered)
    across = jnp.concatenate([gathered] * GROUPS).T
    lanes = block_of_lanes((count, CY))
    result = across[0:count]
    for g in range(1, GROUPS):
        result = jnp.where(lanes == g, across[NZ * g : NZ * g + count], result)
    snap[...] = result


def grid_kernel(block, merged, snap_step, edge, weights_ref, *refs):
    first, last = block == 0, block == len(TILES_Y) - 1
    tiles_y = TILES_Y[block]
    refs = list(refs)
    take = lambda n: [refs.pop(0) for _ in range(n)]
    blocks = [take(1 if merged else 2) for _ in range(3)]
    if first:
        sends = take(1 if TILES_Y[1] < tiles_y else 3)
        shear, bulk = take(2)
    else:
        shear, bulk = take(2)
        if last:
            take(1)
        sends = take(1) if last or TILES_Y[block + 1] < tiles_y else take(3)
    snap = take(1)[0] if snap_step is not None else None
    fields = take(2)

    low_here, high_here = edge[2] == 1, edge[3] == 1
    for i, arrays in enumerate(blocks):
        here = (None, edge[0] == 1, edge[1] == 1)[i]
        sides = [
            side if here is None else jnp.logical_and(here, side)
            for side in (low_here, high_here)
        ]
        targets = [fields[f // 3].at[f % 3] for f in range(6)]
        if first:
            targets = targets + [shear, bulk]
        place_block(
            arrays[0],
            arrays[-1],
            CX * ROWS if merged else 0,
            tiles_y,
            (here, *sides),
            (X0, X0 - CX, X0 + CX)[i],
            targets,
        )

    now, before = fields
    for step in range(1, STEPS + 1):
        advance(step, tiles_y, now, before, shear, bulk, refs, weights_ref)
        now, before = before, now
        if step == snap_step and not last:
            surface_of(now, snap)
    if last:
        whole = sends[0]
        for c in range(3):
            for q in range(CX // 4):
                columns = [now[c, X0 + 4 * q + i, pl.ds(R0, ROWS), :] for i in range(4)]
                grid = jnp.concatenate([pick_block(columns, g) for g in range(GROUPS)]).T
                for i in range(4):
                    x = 4 * q + i
                    rows = grid[NZ * i : NZ * i + NZ]
                    whole[pl.ds(c * NZ * CX + x, NZ, stride=CX), :] = rows
                    snap[CX * c + x : CX * c + x + 1, :] = rows[0:1]
        return
    for f in range(6):
        source = (now, before)[f // 3].at[f % 3]
        for x in range(CX):
            sends[0][f, pl.ds(ROWS * x, ROWS), :] = source[X0 + x, pl.ds(R0, ROWS), :]
        if len(sends) == 1:
            depth, far = tiles_y - 1, sends[0]
            spots = ((R0 - 8 * depth, 0), (R0 + ROWS, GROUPS - 1))
            starts = (CX * ROWS, CX * ROWS + 16 * depth)
            outs = (far, far)
        else:
            depth = TILES_Y[block + 1]
            spots = ((R0 + ROWS - 8 * depth, GROUPS - 1), (R0, 0))
            starts, outs = (0, 0), sends[1:]
        for (row, group), start, out in zip(spots, starts, outs):
            for q in range(CX // 4):
                columns = [source[X0 + 4 * q + i, pl.ds(row, 8 * depth), :] for i in range(4)]
                out[f, pl.ds(start + 8 * depth * q, 8 * depth), :] = pick_block(columns, group)


def run_grid(block, snap_step, edge, weights, blocks, coefs, after=None):
    shape = lambda *s: jax.ShapeDtypeStruct(s, jnp.float32)
    last = block == len(TILES_Y) - 1
    merged = len(blocks[0]) == 1
    if last:
        outs = [shape(3 * NZ * CX, CY)]
    elif TILES_Y[block + 1] < TILES_Y[block]:
        outs = [shape(6, CX * ROWS + 32 * (TILES_Y[block] - 1), 128)]
    else:
        outs = [shape(6, CX * ROWS, 128)] + [shape(6, 16 * TILES_Y[block + 1], 128)] * 2
    operands = [edge, weights] + [array for arrays in blocks for array in arrays]
    if block == 0:
        outs += [shape(XE, RE, 128)] * 2
    else:
        operands += list(coefs)
    specs = [SMEM] + [VMEM] * (len(operands) - 1)
    if last:
        operands.append(after)
        specs.append(HBM)
    if snap_step is not None:
        outs.append(shape(3 * CX, CY))
    field = pltpu.VMEM((3, XE, RE, 128), jnp.float32)
    plane = pltpu.VMEM((XE, RE, 128), jnp.float32)
    return pl.pallas_call(
        functools.partial(grid_kernel, block, merged, snap_step),
        out_shape=outs,
        in_specs=specs,
        out_specs=[VMEM] * len(outs),
        scratch_shapes=[field, field, field, plane, plane, plane, plane],
        compiler_params=pltpu.CompilerParams(vmem_limit_bytes=48 << 20),
        cost_estimate=pl.CostEstimate(
            flops=40_000_000, bytes_accessed=8 << 20, transcendentals=0
        ),
        name="grid_steps",
    )(*operands)


def arrange_kernel(now, before, shear, bulk, own, low, high):
    depth = 8 * TILES_Y[0]
    for f in range(8):
        ref, base = ((now, 256 * f), (before, 256 * (f - 3)), (shear, 0), (bulk, 0))[
            f // 3 if f < 6 else f - 4
        ]
        for q in range(CX // 4):
            values = [ref[pl.ds(base + 4 * q + i, NZ, stride=CX), :] for i in range(4)]
            grid = jnp.concatenate(values).T
            if f >= 6:
                grid = grid * (1.0 / 12.0)
            low[f, pl.ds(depth * q, depth), :] = grid[CY - depth : CY]
            high[f, pl.ds(depth * q, depth), :] = grid[0:depth]
            groups = [grid[ROWS * g : ROWS * g + ROWS] for g in range(GROUPS)]
            for i in range(4):
                own[f, pl.ds(ROWS * (4 * q + i), ROWS), :] = pick_block(groups, i)


def arrange(displacement, previous, shear_coef, bulk_coef):
    shape = lambda *s: jax.ShapeDtypeStruct(s, jnp.float32)
    side = shape(8, 16 * TILES_Y[0], 128)
    flat = [a.reshape(-1, CY) for a in (displacement, previous, shear_coef, bulk_coef)]
    return pl.pallas_call(
        arrange_kernel,
        out_shape=[shape(8, CX * ROWS, 128), side, side],
        in_specs=[VMEM] * 4,
        out_specs=[VMEM] * 3,
        compiler_params=pltpu.CompilerParams(vmem_limit_bytes=24 << 20),
        cost_estimate=pl.CostEstimate(
            flops=1_000_000, bytes_accessed=4 << 20, transcendentals=0
        ),
        name="arrange",
    )(*flat)


def response_kernel(transition, forcing, out, state, total, flipped):
    arch = transition.shape[0]
    for a in range(arch):
        flipped[a] = transition[a].T
    state[...] = jnp.zeros_like(state)
    for a in range(arch):
        state[a, 0:3, :] = forcing[a]

    def one(j, carry):
        for a in range(arch):
            now = state[a]
            total[a] = total[a] + now
            high = now.astype(jnp.bfloat16)
            low = (now - high.astype(jnp.float32)).astype(jnp.bfloat16)
            product = lax.dot_general(
                jnp.concatenate([high, low], axis=0),
                flipped[a],
                (((1,), (0,)), ((), ())),
                preferred_element_type=jnp.float32,
            )
            state[a] = product[0:8] + product[8:16]
        return carry

    for group in range(COUPLINGS):
        moment = COUPLINGS - 1 - group
        total[...] = jnp.zeros_like(total)
        lax.fori_loop(0, SUB, one, 0, unroll=True)
        for a in range(arch):
            for c in range(3):
                for h in range(2):
                    row = 6 * moment + 2 * c + h
                    out[a, row : row + 1, :] = total[a, c : c + 1, 128 * h : 128 * h + 128]
            if SCALES[moment - 1] != SCALES[moment]:
                state[a] = state[a] * (SCALES[moment] / SCALES[moment - 1])


def responses(transition, forcing):
    arch, width = transition.shape[0], transition.shape[1]
    return pl.pallas_call(
        response_kernel,
        out_shape=jax.ShapeDtypeStruct((arch, 6 * COUPLINGS, 128), jnp.float32),
        in_specs=[VMEM, VMEM],
        out_specs=VMEM,
        scratch_shapes=[pltpu.VMEM((arch, 8, width), jnp.float32)] * 2
        + [pltpu.VMEM((arch, width, width), jnp.bfloat16)],
        compiler_params=pltpu.CompilerParams(vmem_limit_bytes=24 << 20),
        cost_estimate=pl.CostEstimate(
            flops=20_000_000, bytes_accessed=2 << 20, transcendentals=0
        ),
        name="responses",
    )(transition, forcing)


def building_kernel(tiles, kinds, place, across, surface, table_ref, *refs):
    before = refs[0] if len(refs) == 5 else None
    out, ground, table, arrived = refs[-4:]
    fetch = pltpu.make_async_copy(
        table_ref.at[:, pl.ds(8 * tiles[0], 8 * len(tiles)), :], table, arrived
    )
    fetch.start()
    count = out.shape[0]
    cells = surface.shape[0] * CY
    picks = (lax.broadcasted_iota(jnp.int32, (cells, count), 0) == place[...]).astype(jnp.bfloat16)
    values = jnp.concatenate([surface[j] for j in range(surface.shape[0])], axis=1)
    high = values.astype(jnp.bfloat16)
    rest = values - high.astype(jnp.float32)
    low = rest.astype(jnp.bfloat16)
    least = (rest - low.astype(jnp.float32)).astype(jnp.bfloat16)
    picked = jnp.dot(
        jnp.concatenate([high, low, least], axis=0), picks, preferred_element_type=jnp.float32
    )
    n = values.shape[0]
    picked = picked[0:n] + picked[n : 2 * n] + picked[2 * n : 3 * n]
    here = lax.broadcasted_iota(jnp.int32, (CX, count), 0) == across[...]
    row = lax.broadcasted_iota(jnp.int32, (8, count), 0)
    first = 4 * tiles[0] // 3 * 3
    for t, tile in enumerate(tiles):
        rows = []
        for k in range(4 * tile, 4 * tile + 4):
            at = CX * (k - first)
            value = jnp.where(here, picked[at : at + CX], 0.0)
            rows.append(jnp.sum(value, axis=0, keepdims=True) * SCALES[k // 3])
        ground[t] = jnp.where(
            row < 4, jnp.where(row < 2, rows[0], rows[1]), jnp.where(row < 6, rows[2], rows[3])
        )
    fetch.wait()

    def some(t, carry):
        base = pl.multiple_of(t * 128, 128)
        motion = [ground[k, :, pl.ds(base, 128)] for k in range(len(tiles))]
        slot = lax.broadcasted_iota(jnp.int32, (8, 128), 0)
        for eight in range(16):
            halves = [jnp.zeros((8, 128), jnp.float32)] * 2
            for k in range(8):
                i = 8 * eight + k
                kind = kinds[base + i]
                total = None
                for j in range(len(tiles)):
                    term = table[kind, 8 * j : 8 * j + 8, :] * jnp.broadcast_to(
                        motion[j][:, i : i + 1], (8, 128)
                    )
                    total = term if total is None else total + term
                total = total + pltpu.roll(total, 4, 0)
                total = total + pltpu.roll(total, 2, 0)
                other = pltpu.roll(total, 1, 0)
                pair = (total, other) if k % 2 == 0 else (other, total)
                halves = [jnp.where(slot == k, new, old) for new, old in zip(pair, halves)]
            rows = pl.ds(base + 8 * eight, 8)
            for h in range(2):
                lanes = slice(128 * h, 128 * h + 128)
                out[rows, lanes] = halves[h] if before is None else halves[h] + before[rows, lanes]
        return carry

    lax.fori_loop(0, count // 128, some, 0)


def building_states(tiles, kinds, place, across, surface, table, width, before=None):
    count = kinds.shape[0]
    more = [] if before is None else [before]
    return pl.pallas_call(
        functools.partial(building_kernel, tiles),
        out_shape=jax.ShapeDtypeStruct((count, width), jnp.float32),
        in_specs=[SMEM] + [VMEM] * 3 + [HBM] + [VMEM] * len(more),
        out_specs=VMEM,
        scratch_shapes=[
            pltpu.VMEM((len(tiles), 8, count), jnp.float32),
            pltpu.VMEM((table.shape[0], 8 * len(tiles), 128), jnp.float32),
            pltpu.SemaphoreType.DMA,
        ],
        compiler_params=pltpu.CompilerParams(vmem_limit_bytes=56 << 20),
        cost_estimate=pl.CostEstimate(
            flops=20_000_000, bytes_accessed=10 << 20, transcendentals=0
        ),
        name="buildings",
    )(kinds, place[None, :], across[None, :], surface, table, *more)


def ring(value, axis, shift):
    count = lax.axis_size(axis)
    return lax.ppermute(value, axis, [(i, (i + shift) % count) for i in range(count)])


def exchange(own, low=None, high=None):
    if low is None:
        return [[own]] + [[ring(own, "slab", shift)] for shift in (1, -1)]
    sides = jnp.concatenate([ring(low, "gy", 1), ring(high, "gy", -1)], axis=1)
    return [[own, sides]] + [
        [ring(own, "slab", shift), ring(sides, "slab", shift)] for shift in (1, -1)
    ]


def per_device(
    displacement, previous, shear_coef, bulk_coef, cell_index, archetype_id, transition, forcing
):
    width = transition.shape[1]
    slab, gy = lax.axis_index("slab"), lax.axis_index("gy")
    slabs, strips = lax.axis_size("slab"), lax.axis_size("gy")
    edge = jnp.stack([slab > 0, slab < slabs - 1, gy > 0, gy < strips - 1]).astype(jnp.int32)
    weights = jnp.asarray(depth_weights(), jnp.bfloat16)

    blocks = exchange(*arrange(displacement, previous, shear_coef, bulk_coef))
    table = lax.all_gather(responses(transition, forcing), ("slab", "gy"), axis=0, tiled=True)

    columns = strips * CY
    along_y = cell_index % columns
    across = cell_index // columns - slab * CX
    place = (gy - along_y // CY) % strips * CY + along_y % CY
    kinds = archetype_id[:, 0]

    def gathered(surface):
        return jnp.stack(
            [surface] + [ring(surface, "gy", shift) for shift in range(1, strips)]
        )

    snaps = []
    coefs = None
    states = None
    count = len(TILES_Y)
    for block in range(count):
        snap_step = next(
            (s for s in range(1, STEPS + 1) if (block * STEPS + s) % EVERY == 0), None
        )
        last = block == count - 1
        if last:
            early = gathered(jnp.concatenate(snaps))
            states = building_states((0, 1), kinds, place, across, early, table, width)
        result = run_grid(block, snap_step, edge, weights, blocks, coefs, states)
        sends = 3 if not last and TILES_Y[block + 1] >= TILES_Y[block] else 1
        if block == 0:
            coefs = result[sends : sends + 2]
        if not last:
            blocks = exchange(*result[:sends])
        if snap_step is not None:
            snaps.append(result[-1])
    final = result[0].reshape(3, NZ, CX, CY)
    late = gathered(snaps[-1])
    recent = jnp.concatenate([early[:, 2 * 3 * CX :], late], axis=1)
    states = building_states((2,), kinds, place, across, recent, table, width, states)
    return (final, states)


def solution(mesh):
    in_specs = (
        P(None, None, "slab", "gy"),
        P(None, None, "slab", "gy"),
        P(None, "slab", "gy"),
        P(None, "slab", "gy"),
        P(("slab", "gy")),
        P(("slab", "gy"), None),
        P(("slab", "gy"), None, None),
        P(("slab", "gy"), None, None),
    )
    out_specs = (P(None, None, "slab", "gy"), P(("slab", "gy"), None))
    return jax.shard_map(
        per_device, mesh=mesh, in_specs=in_specs, out_specs=out_specs, check_vma=False
    )
```

```python
import functools

import jax
import jax.numpy as jnp
import numpy as np
from jax import lax
from jax.experimental import pallas as pl
from jax.experimental.pallas import tpu as pltpu
from jax.sharding import PartitionSpec as P

COUPLINGS = 4
EVERY = 5
SUB = 6
NZ = 32
CX = 8
CY = 128
GROUPS = 4
ROWS = CY // GROUPS
STEPS = 4
X0 = 2 * STEPS + 2
XE = 2 * X0 + CX
TILES_Y = (2, 1, 2, 1, 1)
R0 = 8 * max(TILES_Y) + 8
RE = 2 * R0 + ROWS
CHUNK = 4
SCALES = (2.0**64, 2.0**32, 1.0, 1.0)
VMEM = pl.BlockSpec(memory_space=pltpu.VMEM)
SMEM = pl.BlockSpec(memory_space=pltpu.SMEM)
HBM = pl.BlockSpec(memory_space=pltpu.HBM)


def depth_weights():
    matrix = np.zeros((128, 256), np.float32)
    for lane in range(128):
        base, z = lane // NZ * NZ, lane % NZ
        for k, offset in enumerate(range(-2, 3)):
            source = abs(z + offset)
            if source < NZ:
                matrix[base + source, lane] += (-1, 16, -30, 16, -1)[k]
                matrix[base + source, 128 + lane] += (1, -8, 0, 8, -1)[k]
    return np.concatenate([matrix, matrix])


def block_of_lanes(shape):
    return lax.broadcasted_iota(jnp.int32, shape, len(shape) - 1) // NZ


def turn(value, blocks):
    shift = NZ * (blocks % GROUPS)
    return pltpu.roll(value, shift, 1) if shift else value


def pick_block(values, j):
    lanes = block_of_lanes(values[0].shape)
    result = turn(values[0], 0 - j)
    for i in range(1, GROUPS):
        result = jnp.where(lanes == i, turn(values[i], i - j), result)
    return result


def advance(step, tiles_y, field, former, shear, bulk, scratch, weights_ref):
    second_z, part_x, part_y, first_zx, first_zy = scratch
    halo = 8 * tiles_y
    row_a, tiles_a = R0 - halo - 2 + 2 * step, -(-(ROWS + 2 * halo + 4 - 4 * step) // 8)
    row_b, tiles_b = R0 - halo + 2 * step, -(-(ROWS + 2 * halo - 4 * step) // 8)
    start_a, count_a = 2 * step, XE - 4 * step
    start_b, count_b = start_a + 2, count_a - 4
    height = 8 * tiles_a
    window = pl.ds(row_a, height)

    def firsts(chunk, carry):
        x = start_a + CHUNK * chunk
        along = []
        for c in range(3):
            values = jnp.concatenate([field[c, x + i, window, :] for i in range(CHUNK)])
            high = values.astype(jnp.bfloat16)
            low = (values - high.astype(jnp.float32)).astype(jnp.bfloat16)
            along.append(
                jnp.dot(
                    jnp.concatenate([high, low], axis=1),
                    weights_ref[...],
                    preferred_element_type=jnp.float32,
                )
            )
        along_z = jnp.concatenate(along)
        for i in range(CHUNK):
            for c in range(3):
                at = (CHUNK * c + i) * height
                second_z[c, x + i, window, :] = along_z[at : at + height, 0:128]
            at = i * height
            first_zx[x + i, window, :] = along_z[at : at + height, 128:256]
            at = (CHUNK + i) * height
            first_zy[x + i, window, :] = along_z[at : at + height, 128:256]
        for k in range(tiles_a):
            r = row_a + 8 * k
            rows = pl.ds(r, 8)
            across = [field[0, x + d, rows, :] for d in range(-2, CHUNK + 2)]
            for i in range(CHUNK):
                at = lambda d: field[1, x + i, pl.ds(r + d, 8), :]
                first_y = 8.0 * (at(1) - at(-1)) - (at(2) - at(-2))
                first_x = 8.0 * (across[i + 3] - across[i + 1]) - (across[i + 4] - across[i])
                place = (2 * CHUNK + i) * height + 8 * k
                first_z = along_z[place : place + 8, 128:256]
                part_x[x + i, rows, :] = first_y + first_z
                part_y[x + i, rows, :] = first_x + first_z
        return carry

    def update(chunk, carry):
        x = start_b + CHUNK * chunk
        for k in range(tiles_b):
            r = row_b + 8 * k
            rows = pl.ds(r, 8)

            def first_x(ref):
                across = [ref[x + d, rows, :] for d in range(-2, CHUNK + 2)]
                return [
                    8.0 * (across[i + 3] - across[i + 1]) - (across[i + 4] - across[i])
                    for i in range(CHUNK)
                ]

            def first_y(ref, i):
                at = lambda d: ref[x + i, pl.ds(r + d, 8), :]
                return 8.0 * (at(1) - at(-1)) - (at(2) - at(-2))

            for c in range(3):
                across = [field[c, x + d, rows, :] for d in range(-2, CHUNK + 2)]
                if c == 0:
                    mixed = first_x(part_x)
                elif c == 1:
                    mixed = [first_y(part_y, i) for i in range(CHUNK)]
                else:
                    mixed = [
                        value + first_y(first_zy, i)
                        for i, value in enumerate(first_x(first_zx))
                    ]
                for i in range(CHUNK):
                    at = lambda d: field[c, x + i, pl.ds(r + d, 8), :]
                    centre = across[i + 2]
                    d_x = 16.0 * (across[i + 3] + across[i + 1]) - (across[i + 4] + across[i])
                    d_y = 16.0 * (at(1) + at(-1)) - (at(2) + at(-2))
                    d_z = second_z[c, x + i, rows, :]
                    own = (d_x - 30.0 * centre, d_y - 30.0 * centre, d_z)[c]
                    laplacian = (d_x + d_y) + (d_z - 60.0 * centre)
                    change = shear[x + i, rows, :] * laplacian + bulk[x + i, rows, :] * (
                        own + (1.0 / 12.0) * mixed[i]
                    )
                    former[c, x + i, rows, :] = (
                        2.0 * centre - former[c, x + i, rows, :]
                    ) + change
        return carry

    lax.fori_loop(0, count_a // CHUNK, firsts, 0, unroll=True)
    lax.fori_loop(0, count_b // CHUNK, update, 0)


def place_block(own, halo, halo_from, tiles_y, exists, x_from, targets):
    lanes = block_of_lanes((8, 128))
    here, from_low, from_high = exists

    def keep(flag, value):
        return value if flag is None else jnp.where(flag, value, 0.0)

    def columns(q, carry):
        for f, target in enumerate(targets):
            low, high = [
                [
                    keep(
                        (from_low, from_high)[side],
                        halo[
                            f,
                            pl.ds(
                                pl.multiple_of(
                                    halo_from + 8 * ((2 * side + q) * tiles_y + j), 8
                                ),
                                8,
                            ),
                            :,
                        ],
                    )
                    for j in range(tiles_y)
                ]
                for side in range(2)
            ]
            for i in range(4):
                x = 4 * q + i
                first = pl.multiple_of(ROWS * x, 8)
                tiles = [
                    keep(here, own[f, pl.ds(first + 8 * k, 8), :]) for k in range(ROWS // 8)
                ]
                for k in range(ROWS // 8):
                    target[x_from + x, pl.ds(R0 + 8 * k, 8), :] = tiles[k]
                for j in range(tiles_y):
                    target[x_from + x, pl.ds(R0 + 8 * (j - tiles_y), 8), :] = jnp.where(
                        lanes == 0,
                        turn(low[j], 0 - i),
                        turn(tiles[ROWS // 8 - tiles_y + j], 1),
                    )
                    target[x_from + x, pl.ds(R0 + ROWS + 8 * j, 8), :] = jnp.where(
                        lanes == GROUPS - 1,
                        turn(high[j], GROUPS - 1 - i),
                        turn(tiles[j], GROUPS - 1),
                    )
        return carry

    lax.fori_loop(0, CX // 4, columns, 0)


def surface_of(field, snap):
    count = 3 * CX
    depth = lax.broadcasted_iota(jnp.int32, (ROWS, 128), 1) % NZ
    gathered = field[0, X0, pl.ds(R0, ROWS), :]
    for k in range(1, count):
        layer = pltpu.roll(field[k // CX, X0 + k % CX, pl.ds(R0, ROWS), :], k, 1)
        gathered = jnp.where(depth == k, layer, gathered)
    across = jnp.concatenate([gathered] * GROUPS).T
    lanes = block_of_lanes((count, CY))
    result = across[0:count]
    for g in range(1, GROUPS):
        result = jnp.where(lanes == g, across[NZ * g : NZ * g + count], result)
    snap[...] = result


def grid_kernel(block, merged, snap_step, edge, weights_ref, *refs):
    first, last = block == 0, block == len(TILES_Y) - 1
    tiles_y = TILES_Y[block]
    refs = list(refs)
    take = lambda n: [refs.pop(0) for _ in range(n)]
    blocks = [take(1 if merged else 2) for _ in range(3)]
    if first:
        sends = take(1 if TILES_Y[1] < tiles_y else 3)
        shear, bulk = take(2)
    else:
        shear, bulk = take(2)
        if last:
            take(1)
        sends = take(1) if last or TILES_Y[block + 1] < tiles_y else take(3)
    snap = take(1)[0] if snap_step is not None else None
    fields = take(2)

    low_here, high_here = edge[2] == 1, edge[3] == 1
    for i, arrays in enumerate(blocks):
        here = (None, edge[0] == 1, edge[1] == 1)[i]
        sides = [
            side if here is None else jnp.logical_and(here, side)
            for side in (low_here, high_here)
        ]
        targets = [fields[f // 3].at[f % 3] for f in range(6)]
        if first:
            targets = targets + [shear, bulk]
        place_block(
            arrays[0],
            arrays[-1],
            CX * ROWS if merged else 0,
            tiles_y,
            (here, *sides),
            (X0, X0 - CX, X0 + CX)[i],
            targets,
        )

    now, before = fields
    for step in range(1, STEPS + 1):
        advance(step, tiles_y, now, before, shear, bulk, refs, weights_ref)
        now, before = before, now
        if step == snap_step and not last:
            surface_of(now, snap)
    if last:
        whole = sends[0]
        for c in range(3):
            for q in range(CX // 4):
                columns = [now[c, X0 + 4 * q + i, pl.ds(R0, ROWS), :] for i in range(4)]
                grid = jnp.concatenate([pick_block(columns, g) for g in range(GROUPS)]).T
                for i in range(4):
                    x = 4 * q + i
                    rows = grid[NZ * i : NZ * i + NZ]
                    whole[pl.ds(c * NZ * CX + x, NZ, stride=CX), :] = rows
                    snap[CX * c + x : CX * c + x + 1, :] = rows[0:1]
        return
    for f in range(6):
        source = (now, before)[f // 3].at[f % 3]
        for x in range(CX):
            sends[0][f, pl.ds(ROWS * x, ROWS), :] = source[X0 + x, pl.ds(R0, ROWS), :]
        if len(sends) == 1:
            depth, far = tiles_y - 1, sends[0]
            spots = ((R0 - 8 * depth, 0), (R0 + ROWS, GROUPS - 1))
            starts = (CX * ROWS, CX * ROWS + 16 * depth)
            outs = (far, far)
        else:
            depth = TILES_Y[block + 1]
            spots = ((R0 + ROWS - 8 * depth, GROUPS - 1), (R0, 0))
            starts, outs = (0, 0), sends[1:]
        for (row, group), start, out in zip(spots, starts, outs):
            for q in range(CX // 4):
                columns = [source[X0 + 4 * q + i, pl.ds(row, 8 * depth), :] for i in range(4)]
                out[f, pl.ds(start + 8 * depth * q, 8 * depth), :] = pick_block(columns, group)


def run_grid(block, snap_step, edge, weights, blocks, coefs, after=None):
    shape = lambda *s: jax.ShapeDtypeStruct(s, jnp.float32)
    last = block == len(TILES_Y) - 1
    merged = len(blocks[0]) == 1
    if last:
        outs = [shape(3 * NZ * CX, CY)]
    elif TILES_Y[block + 1] < TILES_Y[block]:
        outs = [shape(6, CX * ROWS + 32 * (TILES_Y[block] - 1), 128)]
    else:
        outs = [shape(6, CX * ROWS, 128)] + [shape(6, 16 * TILES_Y[block + 1], 128)] * 2
    operands = [edge, weights] + [array for arrays in blocks for array in arrays]
    if block == 0:
        outs += [shape(XE, RE, 128)] * 2
    else:
        operands += list(coefs)
    specs = [SMEM] + [VMEM] * (len(operands) - 1)
    if last:
        operands.append(after)
        specs.append(HBM)
    if snap_step is not None:
        outs.append(shape(3 * CX, CY))
    field = pltpu.VMEM((3, XE, RE, 128), jnp.float32)
    plane = pltpu.VMEM((XE, RE, 128), jnp.float32)
    return pl.pallas_call(
        functools.partial(grid_kernel, block, merged, snap_step),
        out_shape=outs,
        in_specs=specs,
        out_specs=[VMEM] * len(outs),
        scratch_shapes=[field, field, field, plane, plane, plane, plane],
        compiler_params=pltpu.CompilerParams(vmem_limit_bytes=48 << 20),
        cost_estimate=pl.CostEstimate(
            flops=40_000_000, bytes_accessed=8 << 20, transcendentals=0
        ),
        name="grid_steps",
    )(*operands)


def arrange_kernel(now, before, shear, bulk, own, low, high):
    depth = 8 * TILES_Y[0]
    for f in range(8):
        ref, base = ((now, 256 * f), (before, 256 * (f - 3)), (shear, 0), (bulk, 0))[
            f // 3 if f < 6 else f - 4
        ]
        for q in range(CX // 4):
            values = [ref[pl.ds(base + 4 * q + i, NZ, stride=CX), :] for i in range(4)]
            grid = jnp.concatenate(values).T
            if f >= 6:
                grid = grid * (1.0 / 12.0)
            low[f, pl.ds(depth * q, depth), :] = grid[CY - depth : CY]
            high[f, pl.ds(depth * q, depth), :] = grid[0:depth]
            groups = [grid[ROWS * g : ROWS * g + ROWS] for g in range(GROUPS)]
            for i in range(4):
                own[f, pl.ds(ROWS * (4 * q + i), ROWS), :] = pick_block(groups, i)


def arrange(displacement, previous, shear_coef, bulk_coef):
    shape = lambda *s: jax.ShapeDtypeStruct(s, jnp.float32)
    side = shape(8, 16 * TILES_Y[0], 128)
    flat = [a.reshape(-1, CY) for a in (displacement, previous, shear_coef, bulk_coef)]
    return pl.pallas_call(
        arrange_kernel,
        out_shape=[shape(8, CX * ROWS, 128), side, side],
        in_specs=[VMEM] * 4,
        out_specs=[VMEM] * 3,
        compiler_params=pltpu.CompilerParams(vmem_limit_bytes=24 << 20),
        cost_estimate=pl.CostEstimate(
            flops=1_000_000, bytes_accessed=4 << 20, transcendentals=0
        ),
        name="arrange",
    )(*flat)


def response_kernel(transition, forcing, out, state, total, flipped):
    arch = transition.shape[0]
    for a in range(arch):
        flipped[a] = transition[a].T
    state[...] = jnp.zeros_like(state)
    for a in range(arch):
        state[a, 0:3, :] = forcing[a]

    def one(j, carry):
        for a in range(arch):
            now = state[a]
            total[a] = total[a] + now
            high = now.astype(jnp.bfloat16)
            low = (now - high.astype(jnp.float32)).astype(jnp.bfloat16)
            product = lax.dot_general(
                jnp.concatenate([high, low], axis=0),
                flipped[a],
                (((1,), (0,)), ((), ())),
                preferred_element_type=jnp.float32,
            )
            state[a] = product[0:8] + product[8:16]
        return carry

    for group in range(COUPLINGS):
        moment = COUPLINGS - 1 - group
        total[...] = jnp.zeros_like(total)
        lax.fori_loop(0, SUB, one, 0, unroll=True)
        for a in range(arch):
            for c in range(3):
                for h in range(2):
                    row = 6 * moment + 2 * c + h
                    out[a, row : row + 1, :] = total[a, c : c + 1, 128 * h : 128 * h + 128]
            if SCALES[moment - 1] != SCALES[moment]:
                state[a] = state[a] * (SCALES[moment] / SCALES[moment - 1])


def responses(transition, forcing):
    arch, width = transition.shape[0], transition.shape[1]
    return pl.pallas_call(
        response_kernel,
        out_shape=jax.ShapeDtypeStruct((arch, 6 * COUPLINGS, 128), jnp.float32),
        in_specs=[VMEM, VMEM],
        out_specs=VMEM,
        scratch_shapes=[pltpu.VMEM((arch, 8, width), jnp.float32)] * 2
        + [pltpu.VMEM((arch, width, width), jnp.bfloat16)],
        compiler_params=pltpu.CompilerParams(vmem_limit_bytes=24 << 20),
        cost_estimate=pl.CostEstimate(
            flops=20_000_000, bytes_accessed=2 << 20, transcendentals=0
        ),
        name="responses",
    )(transition, forcing)


def building_kernel(tiles, kinds, place, across, surface, table_ref, *refs):
    before = refs[0] if len(refs) == 5 else None
    out, ground, table, arrived = refs[-4:]
    fetch = pltpu.make_async_copy(
        table_ref.at[:, pl.ds(8 * tiles[0], 8 * len(tiles)), :], table, arrived
    )
    fetch.start()
    count = out.shape[0]
    cells = surface.shape[0] * CY
    picks = (lax.broadcasted_iota(jnp.int32, (cells, count), 0) == place[...]).astype(jnp.bfloat16)
    values = jnp.concatenate([surface[j] for j in range(surface.shape[0])], axis=1)
    high = values.astype(jnp.bfloat16)
    rest = values - high.astype(jnp.float32)
    low = rest.astype(jnp.bfloat16)
    least = (rest - low.astype(jnp.float32)).astype(jnp.bfloat16)
    picked = jnp.dot(
        jnp.concatenate([high, low, least], axis=0), picks, preferred_element_type=jnp.float32
    )
    n = values.shape[0]
    picked = picked[0:n] + picked[n : 2 * n] + picked[2 * n : 3 * n]
    here = lax.broadcasted_iota(jnp.int32, (CX, count), 0) == across[...]
    row = lax.broadcasted_iota(jnp.int32, (8, count), 0)
    first = 4 * tiles[0] // 3 * 3
    for t, tile in enumerate(tiles):
        rows = []
        for k in range(4 * tile, 4 * tile + 4):
            at = CX * (k - first)
            value = jnp.where(here, picked[at : at + CX], 0.0)
            rows.append(jnp.sum(value, axis=0, keepdims=True) * SCALES[k // 3])
        ground[t] = jnp.where(
            row < 4, jnp.where(row < 2, rows[0], rows[1]), jnp.where(row < 6, rows[2], rows[3])
        )
    fetch.wait()

    def some(t, carry):
        base = pl.multiple_of(t * 128, 128)
        motion = [ground[k, :, pl.ds(base, 128)] for k in range(len(tiles))]
        slot = lax.broadcasted_iota(jnp.int32, (8, 128), 0)
        for eight in range(16):
            halves = [jnp.zeros((8, 128), jnp.float32)] * 2
            for k in range(8):
                i = 8 * eight + k
                kind = kinds[base + i]
                total = None
                for j in range(len(tiles)):
                    term = table[kind, 8 * j : 8 * j + 8, :] * jnp.broadcast_to(
                        motion[j][:, i : i + 1], (8, 128)
                    )
                    total = term if total is None else total + term
                total = total + pltpu.roll(total, 4, 0)
                total = total + pltpu.roll(total, 2, 0)
                other = pltpu.roll(total, 1, 0)
                pair = (total, other) if k % 2 == 0 else (other, total)
                halves = [jnp.where(slot == k, new, old) for new, old in zip(pair, halves)]
            rows = pl.ds(base + 8 * eight, 8)
            for h in range(2):
                lanes = slice(128 * h, 128 * h + 128)
                out[rows, lanes] = halves[h] if before is None else halves[h] + before[rows, lanes]
        return carry

    lax.fori_loop(0, count // 128, some, 0)


def building_states(tiles, kinds, place, across, surface, table, width, before=None):
    count = kinds.shape[0]
    more = [] if before is None else [before]
    return pl.pallas_call(
        functools.partial(building_kernel, tiles),
        out_shape=jax.ShapeDtypeStruct((count, width), jnp.float32),
        in_specs=[SMEM] + [VMEM] * 3 + [HBM] + [VMEM] * len(more),
        out_specs=VMEM,
        scratch_shapes=[
            pltpu.VMEM((len(tiles), 8, count), jnp.float32),
            pltpu.VMEM((table.shape[0], 8 * len(tiles), 128), jnp.float32),
            pltpu.SemaphoreType.DMA,
        ],
        compiler_params=pltpu.CompilerParams(vmem_limit_bytes=56 << 20),
        cost_estimate=pl.CostEstimate(
            flops=20_000_000, bytes_accessed=10 << 20, transcendentals=0
        ),
        name="buildings",
    )(kinds, place[None, :], across[None, :], surface, table, *more)


def ring(value, axis, shift):
    count = lax.axis_size(axis)
    return lax.ppermute(value, axis, [(i, (i + shift) % count) for i in range(count)])


def exchange(own, low=None, high=None):
    if low is None:
        return [[own]] + [[ring(own, "slab", shift)] for shift in (1, -1)]
    sides = jnp.concatenate([ring(low, "gy", 1), ring(high, "gy", -1)], axis=1)
    return [[own, sides]] + [
        [ring(own, "slab", shift), ring(sides, "slab", shift)] for shift in (1, -1)
    ]


def per_device(
    displacement, previous, shear_coef, bulk_coef, cell_index, archetype_id, transition, forcing
):
    width = transition.shape[1]
    slab, gy = lax.axis_index("slab"), lax.axis_index("gy")
    slabs, strips = lax.axis_size("slab"), lax.axis_size("gy")
    edge = jnp.stack([slab > 0, slab < slabs - 1, gy > 0, gy < strips - 1]).astype(jnp.int32)
    weights = jnp.asarray(depth_weights(), jnp.bfloat16)

    blocks = exchange(*arrange(displacement, previous, shear_coef, bulk_coef))
    table = lax.all_gather(responses(transition, forcing), ("slab", "gy"), axis=0, tiled=True)

    columns = strips * CY
    along_y = cell_index % columns
    across = cell_index // columns - slab * CX
    place = (gy - along_y // CY) % strips * CY + along_y % CY
    kinds = archetype_id[:, 0]

    def gathered(surface):
        return jnp.stack(
            [surface] + [ring(surface, "gy", shift) for shift in range(1, strips)]
        )

    snaps = []
    coefs = None
    states = None
    count = len(TILES_Y)
    for block in range(count):
        snap_step = next(
            (s for s in range(1, STEPS + 1) if (block * STEPS + s) % EVERY == 0), None
        )
        last = block == count - 1
        if last:
            early = gathered(jnp.concatenate(snaps))
            states = building_states((0, 1), kinds, place, across, early, table, width)
        result = run_grid(block, snap_step, edge, weights, blocks, coefs, states)
        sends = 3 if not last and TILES_Y[block + 1] >= TILES_Y[block] else 1
        if block == 0:
            coefs = result[sends : sends + 2]
        if not last:
            blocks = exchange(*result[:sends])
        if snap_step is not None:
            snaps.append(result[-1])
    final = result[0].reshape(3, NZ, CX, CY)
    late = gathered(snaps[-1])
    recent = jnp.concatenate([early[:, 2 * 3 * CX :], late], axis=1)
    states = building_states((2,), kinds, place, across, recent, table, width, states)
    return (final, states)


def solution(mesh):
    in_specs = (
        P(None, None, "slab", "gy"),
        P(None, None, "slab", "gy"),
        P(None, "slab", "gy"),
        P(None, "slab", "gy"),
        P(("slab", "gy")),
        P(("slab", "gy"), None),
        P(("slab", "gy"), None, None),
        P(("slab", "gy"), None, None),
    )
    out_specs = (P(None, None, "slab", "gy"), P(("slab", "gy"), None))
    return jax.shard_map(
        per_device, mesh=mesh, in_specs=in_specs, out_specs=out_specs, check_vma=False
    )
```
